128 devices in a mesh: dp: 16 (over x, y_hi, core), tensor: 8 (over y_lo, z).
Axes of the slice: x: 4, y: 4 (y_hi: 2, y_lo: 2; y = y_hi * 2 + y_lo), z: 4, core: 2. Of those that a mesh axis runs over, the one named last changes fastest.
Arguments:
- wide_up: bfloat16 [4096, 16384], P(None, 'dp'), may hold values from -0.09375 to 0.09375
- wide_down: bfloat16 [16384, 4096], P('dp'), may hold values from -0.046875 to 0.046875
- narrow_up: bfloat16 [4096, 4096], P('dp', 'tensor'), may hold values from -0.09375 to 0.09375
- narrow_down: bfloat16 [4096, 4096], P('tensor', 'dp'), may hold values from -0.09375 to 0.09375
- wide_input: bfloat16 [2048, 4096], P('tensor'), may hold values from -6 to 6
- wide_preact: bfloat16 [2048, 16384], P('tensor', 'dp'), may hold values from -8 to 8
- narrow_input: bfloat16 [2048, 4096], P('dp'), may hold values from -6 to 6
- narrow_preact: bfloat16 [2048, 4096], P('dp', 'tensor'), may hold values from -8 to 8
- cotangent: bfloat16 [2048, 4096], P('dp', 'tensor'), may hold values from -6 to 6
Outputs:
- wide_input_grad: bfloat16 [2048, 4096], P('tensor', 'dp')
- wide_up_grad: bfloat16 [4096, 16384], P('tensor', 'dp')
- wide_down_grad: bfloat16 [16384, 4096], P('dp', 'tensor')
- narrow_up_grad: bfloat16 [4096, 4096], P('dp', 'tensor')
- narrow_down_grad: bfloat16 [4096, 4096], P('tensor', 'dp')
The draws below stay inside these ranges and needn't reach their ends.
All inputs are finite; a program needn't handle non-finite values.
Results may differ from the reference program's by a relative error of at most 0.025.
Values may be sent and summed in bfloat16 or wider, within the bound.
No kernel may reach another device: no remote copies, remote signals or barrier semaphores. Data moves between devices by JAX's collectives and lax.ppermute only.
A program may use at most 128 MiB of HBM per device.

```python
import jax
import jax.numpy as jnp
from jax import lax

D = 4096
FW = 16384
FN = 4096
TOKENS = 2048
N_DP = 16
N_TENSOR = 8


def block_scale(key, shape, pieces, low, top_value):
    loudness = 1.0
    for position, shards_of in pieces:
        heights = jax.random.uniform(jax.random.fold_in(jax.random.fold_in(key, 6), position), (shards_of,), jnp.float32, low / len(pieces), top_value / len(pieces))
        loudness = loudness * jnp.repeat(jnp.exp(heights), shape[position] // shards_of).reshape((-1,) + (1,) * (len(shape) - 1 - position))
    return loudness


def normal_values(stream_key, dims, spread, bound, shards=(), held_as=jnp.bfloat16):
    level = block_scale(stream_key, dims, shards, -0.22, 0.18) if shards else 1.0
    entries = jax.random.normal(stream_key, dims, jnp.float32) * spread * level
    return jnp.minimum(jnp.maximum(entries, -bound), bound).astype(held_as)


def setup_inputs(seed: int = 0) -> dict:
    seeds = jax.random.split(jax.random.key(seed), 10)
    wide_up = normal_values(seeds[0], (D, FW), D ** -0.5, 0.09375, ((1, 16),))
    wide_down = normal_values(seeds[1], (FW, D), FW ** -0.5, 0.046875, ((0, 16),))
    narrow_up = normal_values(seeds[2], (D, FN), D ** -0.5, 0.09375, ((0, 16), (1, 8)))
    narrow_down = normal_values(seeds[3], (FN, D), FN ** -0.5, 0.09375, ((0, 8), (1, 16)))
    wide_input = normal_values(seeds[4], (TOKENS, D), 1.0, 6.0, ((0, 8),))
    wide_preact = normal_values(seeds[5], (TOKENS, FW), 1.5, 8.0, ((0, 8), (1, 16)))
    narrow_input = normal_values(seeds[6], (TOKENS, D), 1.0, 6.0, ((0, 16),))
    narrow_preact = normal_values(seeds[7], (TOKENS, FN), 1.5, 8.0, ((0, 16), (1, 8)))
    cotangent = normal_values(seeds[8], (TOKENS, D), 1.0, 6.0, ((0, 16), (1, 8)))
    return dict(wide_up=wide_up, wide_down=wide_down, narrow_up=narrow_up, narrow_down=narrow_down, wide_input=wide_input, wide_preact=wide_preact, narrow_input=narrow_input, narrow_preact=narrow_preact, cotangent=cotangent)


def silu_slope(values):
    sig = jax.nn.sigmoid(values)
    return sig * (1.0 + values * (1.0 - sig))

def blocked_grad(left, right, blocks):
    left_blocks = left.reshape(blocks, -1, left.shape[1])
    right_blocks = right.reshape(blocks, -1, right.shape[1])

    def accumulate(running, pair):
        term = jnp.dot(pair[0].T, pair[1], preferred_element_type=jnp.float32)
        rounded = lax.optimization_barrier(term.astype(jnp.bfloat16)).astype(jnp.float32)
        return (running + rounded, None)
    start_value = jnp.zeros((left.shape[1], right.shape[1]), jnp.float32)
    running, unused = lax.scan(accumulate, start_value, (left_blocks, right_blocks))
    return running.astype(jnp.bfloat16)

def reference(wide_up, wide_down, narrow_up, narrow_down, wide_input, wide_preact, narrow_input, narrow_preact, cotangent):
    narrow_hidden_grad = jnp.dot(cotangent, narrow_down.T, preferred_element_type=jnp.float32)
    narrow_pre = narrow_preact.astype(jnp.float32)
    narrow_act = jax.nn.silu(narrow_pre).astype(jnp.bfloat16)
    narrow_down_grad = blocked_grad(narrow_act, cotangent, N_DP)
    narrow_pre_grad = (narrow_hidden_grad * silu_slope(narrow_pre)).astype(jnp.bfloat16)
    narrow_up_grad = blocked_grad(narrow_input, narrow_pre_grad, N_DP)
    boundary_grad = (cotangent.astype(jnp.float32) + jnp.dot(narrow_pre_grad, narrow_up.T, preferred_element_type=jnp.float32)).astype(jnp.bfloat16)
    wide_hidden_grad = jnp.dot(boundary_grad, wide_down.T, preferred_element_type=jnp.float32)
    wide_pre = wide_preact.astype(jnp.float32)
    wide_act = jax.nn.silu(wide_pre).astype(jnp.bfloat16)
    wide_down_grad = blocked_grad(wide_act, boundary_grad, N_TENSOR)
    wide_pre_grad = (wide_hidden_grad * silu_slope(wide_pre)).astype(jnp.bfloat16)
    wide_up_grad = blocked_grad(wide_input, wide_pre_grad, N_TENSOR)
    wide_input_grad = (boundary_grad.astype(jnp.float32) + jnp.dot(wide_pre_grad, wide_up.T, preferred_element_type=jnp.float32)).astype(jnp.bfloat16)
    return (wide_input_grad, wide_up_grad, wide_down_grad, narrow_up_grad, narrow_down_grad)
```

```python
import jax
import jax.numpy as jnp
from jax import lax
from jax.sharding import Mesh, PartitionSpec as P

BF16 = jnp.bfloat16
F32 = jnp.float32
CHIPS = ("x", "yh")
TOK = ("yl", "z")


def silu_slope(values):
    sig = jax.nn.sigmoid(values)
    return sig * (1.0 + values * (1.0 - sig))


def dot(left, right, dims):
    return lax.dot_general(left, right, (dims, ((), ())), preferred_element_type=F32)


def swap_cores(value):
    return lax.ppermute(value, "c", [(0, 1), (1, 0)])


def swap_pair(value):
    return lax.ppermute(value, "yl", [(0, 1), (1, 0)])


def shift_z(value, by):
    return lax.ppermute(value, "z", [(i, (i + by) % 4) for i in range(4)])


def exchange(value, axes):
    return lax.all_to_all(value, axes, 0, 0, tiled=True)


def gather_all(value, axes, count):
    return exchange(jnp.broadcast_to(value[None], (count,) + value.shape), axes)


def pick(value, index, axis):
    return lax.dynamic_index_in_dim(value, index, axis, keepdims=False)


def z_columns(rows, z, core):
    cols = rows.reshape(rows.shape[0], 2, 4, -1)
    half = rows.shape[0] // 2
    own = pick(cols, z, 2).reshape(rows.shape[0], -1)
    mine = lax.dynamic_slice_in_dim(cols, core * half, half, 0)
    got = []
    for by in (1, 3, 2):
        got.append(shift_z(pick(mine, (z + by) % 4, 2).reshape(half, -1), by))
    got = jnp.stack(got)
    other = swap_cores(got)
    first = jnp.where(core == 0, got, other)
    second = jnp.where(core == 0, other, got)
    both = jnp.concatenate([first, second], axis=1)
    return jnp.concatenate([own[None], both]).reshape(4 * rows.shape[0], -1)


def z_rows(block):
    return jnp.concatenate([block] + [shift_z(block, by) for by in (1, 3, 2)])


def body(
    wide_up,
    wide_down,
    narrow_up,
    narrow_down,
    wide_input,
    wide_preact,
    narrow_input,
    narrow_preact,
    cotangent,
):
    core = lax.axis_index("c")
    z = lax.axis_index("z")
    yl = lax.axis_index("yl")
    chip = lax.axis_index("x") * 2 + lax.axis_index("yh")
    tok = yl * 4 + z
    tokens, width = cotangent.shape
    n_t, n_d = 8, 8
    half = narrow_down.shape[1]

    cot_rows = gather_all(cotangent, TOK, n_t)
    down_cols = gather_all(narrow_down, CHIPS, n_d)
    cot_cols = cot_rows.reshape(n_d, tokens, 2, half)
    keep = pick(cot_cols, core, 2)
    come = swap_cores(pick(cot_cols, 1 - core, 2))
    pre_f = narrow_preact.astype(F32)
    hid_keep = jnp.einsum("dtk,dfk->tf", keep, down_cols, preferred_element_type=F32)
    hid_send = jnp.einsum("dtk,dfk->tf", come, down_cols, preferred_element_type=F32)
    hidden_grad = hid_keep + swap_cores(hid_send)
    narrow_pre_grad = (hidden_grad * silu_slope(pre_f)).astype(BF16)

    pre_all = gather_all(narrow_pre_grad, CHIPS, n_d).reshape(n_d * tokens, -1)
    act_all = gather_all(jax.nn.silu(pre_f).astype(BF16), CHIPS, n_d).reshape(n_d * tokens, -1)
    cot_own = exchange(cot_rows, CHIPS)
    in_own = exchange(
        narrow_input.reshape(tokens, n_d, -1).transpose(1, 0, 2), CHIPS
    ).reshape(n_d * tokens, -1)

    up_other = swap_cores(narrow_up)
    up_first = jnp.where(core == 0, narrow_up, up_other)
    up_second = jnp.where(core == 0, up_other, narrow_up)
    up_rows = jnp.concatenate([up_first, up_second])
    share = dot(pre_all, up_rows, ((1,), (1,))).astype(BF16)
    share = exchange(share.reshape(n_t, tokens, -1), TOK)
    own = pick(cot_own, tok, 0).astype(F32) + jnp.sum(share.astype(F32), axis=0)
    own = own.astype(BF16)
    rows = gather_all(own, CHIPS, n_d).transpose(1, 0, 2).reshape(tokens, -1)
    rows_other = swap_cores(rows)
    boundary = jnp.concatenate(
        [jnp.where(core == 0, rows, rows_other), jnp.where(core == 0, rows_other, rows)]
    )

    wide_pre = wide_preact.astype(F32)
    wide_hidden_grad = dot(boundary, wide_down, ((1,), (1,)))
    wide_pre_grad = (wide_hidden_grad * silu_slope(wide_pre)).astype(BF16)
    term = dot(wide_pre_grad, wide_up, ((1,), (1,)))
    term = term.reshape(2 * tokens, n_d, 2, half)
    term_keep = pick(term, core, 2)
    term_come = swap_cores(pick(term, 1 - core, 2).astype(BF16))
    term_chip = (term_keep + term_come.astype(F32)).astype(BF16).transpose(1, 0, 2)
    term_all = exchange(term_chip, CHIPS)
    own_cols = lax.dynamic_slice_in_dim(boundary, (chip * 2 + core) * half, half, 1)
    wide_input_grad = (own_cols.astype(F32) + jnp.sum(term_all.astype(F32), axis=0)).astype(BF16)

    wide_act = jax.nn.silu(wide_pre).astype(BF16)
    act_rows = z_rows(wide_act)
    bound_cols = z_columns(boundary, z, core)
    input_cols = z_columns(wide_input, z, core)
    grad_rows = z_rows(wide_pre_grad)
    side = bound_cols.shape[1] // 2

    def take(cols, which):
        return lax.dynamic_slice_in_dim(cols, which * side, side, 1)

    down_send = dot(act_rows, take(bound_cols, 1 - yl), ((0,), (0,))).astype(BF16)
    down_come = swap_pair(down_send)
    down_keep = dot(act_rows, take(bound_cols, yl), ((0,), (0,)))
    wide_down_grad = (down_keep + down_come.astype(F32)).astype(BF16)
    up_send = dot(take(input_cols, 1 - yl), grad_rows, ((0,), (0,))).astype(BF16)
    up_come = swap_pair(up_send)
    up_keep = dot(take(input_cols, yl), grad_rows, ((0,), (0,)))
    wide_up_grad = (up_keep + up_come.astype(F32)).astype(BF16)

    cot_tok = cot_own.reshape(n_d * tokens, -1)

    def core_sum(part, axis):
        size = part.shape[axis] // 2
        send = lax.dynamic_slice_in_dim(part, (1 - core) * size, size, axis).astype(BF16)
        mine = lax.dynamic_slice_in_dim(part, core * size, size, axis)
        return (mine + swap_cores(send).astype(F32)).astype(BF16)

    narrow_down_grad = core_sum(dot(act_all, cot_tok, ((0,), (0,))), 1)
    narrow_up_grad = core_sum(dot(in_own, pre_all, ((0,), (0,))), 0)
    return (wide_input_grad, wide_up_grad, wide_down_grad, narrow_up_grad, narrow_down_grad)


def solution(mesh):
    fine = Mesh(mesh.devices.reshape(4, 2, 2, 2, 4), ("x", "yh", "c", "yl", "z"))
    dp = ("x", "yh", "c")
    tensor = ("yl", "z")
    in_specs = (
        P(None, dp),
        P(dp, None),
        P(dp, tensor),
        P(tensor, dp),
        P(tensor, None),
        P(tensor, dp),
        P(dp, None),
        P(dp, tensor),
        P(dp, tensor),
    )
    out_specs = (
        P(tensor, dp),
        P(tensor, dp),
        P(dp, tensor),
        P(dp, tensor),
        P(tensor, dp),
    )
    return jax.shard_map(body, mesh=fine, in_specs=in_specs, out_specs=out_specs, check_vma=False)
```

```python
import jax
import jax.numpy as jnp
from jax import lax
from jax.experimental import pallas as pl
from jax.experimental.pallas import tpu as pltpu
from jax.sharding import Mesh, PartitionSpec as P

BF16 = jnp.bfloat16
F32 = jnp.float32
CHIPS = ("x", "yh")
TOK = ("yl", "z")


def silu_slope(values):
    sig = jax.nn.sigmoid(values)
    return sig * (1.0 + values * (1.0 - sig))


def dot(left, right, dims):
    return lax.dot_general(left, right, (dims, ((), ())), preferred_element_type=F32)


def flip(value, axis, by=1):
    size = lax.axis_size(axis)
    return lax.ppermute(value, axis, [(i, i ^ by) for i in range(size)])


def exchange(value, axes):
    return lax.all_to_all(value, axes, 0, 0, tiled=True)


def gather_all(value, axes, count):
    return exchange(jnp.broadcast_to(value[None], (count,) + value.shape), axes)


def pick(value, index, axis):
    return lax.dynamic_index_in_dim(value, index, axis, keepdims=False)


def cut(value, start, size, axis):
    return lax.dynamic_slice_in_dim(value, start, size, axis)


def after(value, *others):
    return lax.optimization_barrier((value,) + others)[0]


def z_columns(rows, yl, z, core, side):
    group = jnp.where(core == 0, yl, 1 - yl)
    got = [flip(cut(rows, (group * 4 + (z ^ by)) * side, side, 1), "z", by) for by in (1, 2, 3)]
    got = jnp.concatenate(got)
    come = flip(got, "c")
    own = jnp.concatenate([cut(rows, (yl * 4 + z) * side, side, 1), jnp.where(core == 0, got, come)])
    pair = jnp.concatenate([cut(rows, ((1 - yl) * 4 + z) * side, side, 1), jnp.where(core == 0, come, got)])
    return own, pair


def z_rows(block):
    return jnp.concatenate([block] + [flip(block, "z", by) for by in (1, 2, 3)])


def chip_blocks(blocks, x, yh):
    four = blocks.reshape((4, 2) + blocks.shape[1:])
    pair = jnp.stack([pick(four, yh, 1), flip(pick(four, 1 - yh, 1), "yh")])
    out = [pick(pair, x, 1)] + [flip(pick(pair, x ^ by, 1), "x", by) for by in (1, 2, 3)]
    return jnp.concatenate(out)


def term_kernel(parity_ref, grad_ref, up_ref, *rest):
    out_ref = rest[-1]
    part = lax.dot_general(
        grad_ref[...], up_ref[...], (((1,), (1,)), ((), ())), preferred_element_type=F32
    )
    for add in rest[:-1]:
        part = part + add[0].astype(F32)
    out_ref[0] = part.astype(BF16)


def term_blocks(grad, up, parity, half, add=()):
    rows, depth = grad.shape
    count = up.shape[0] // (2 * half)
    block = pl.BlockSpec((1, rows, half), lambda i, par: (i, 0, 0))
    return pl.pallas_call(
        term_kernel,
        grid_spec=pltpu.PrefetchScalarGridSpec(
            num_scalar_prefetch=1,
            grid=(count,),
            in_specs=[
                pl.BlockSpec((rows, depth), lambda i, par: (0, 0)),
                pl.BlockSpec((half, depth), lambda i, par: (2 * i + par[0], 0)),
            ]
            + [block] * len(add),
            out_specs=block,
        ),
        out_shape=jax.ShapeDtypeStruct((count, rows, half), BF16),
        cost_estimate=pl.CostEstimate(
            flops=2 * count * rows * half * depth,
            bytes_accessed=2 * count * half * depth,
            transcendentals=0,
        ),
        compiler_params=pltpu.CompilerParams(vmem_limit_bytes=16 * 1024 * 1024),
        name="term",
    )(parity.reshape(1).astype(jnp.int32), grad, up, *add)


def body(
    wide_up,
    wide_down,
    narrow_up,
    narrow_down,
    wide_input,
    wide_preact,
    narrow_input,
    narrow_preact,
    cotangent,
):
    core = lax.axis_index("c")
    z = lax.axis_index("z")
    yl = lax.axis_index("yl")
    x = lax.axis_index("x")
    yh = lax.axis_index("yh")
    chip = x * 2 + yh
    tok = yl * 4 + z
    tokens, side = cotangent.shape
    n_t, n_d = 8, 8
    half = narrow_down.shape[1]

    wide_pre = wide_preact.astype(F32)
    wide_act = jax.nn.silu(wide_pre).astype(BF16)
    act_all = lax.all_gather(wide_act, TOK, axis=0, tiled=True)

    down_copies = jnp.broadcast_to(narrow_down[None], (n_d,) + narrow_down.shape)
    down_cols = exchange(down_copies, CHIPS)
    cot = after(cotangent, down_copies)
    near = jnp.stack([cot, flip(cot, "yl")])
    near = jnp.stack([near] + [flip(near, "z", by) for by in (1, 2, 3)])
    near = near.reshape(n_t, tokens, side)
    cot_rows = jnp.stack([pick(near, (z ^ (i % 4)) * 2 + (yl ^ (i // 4)), 0) for i in range(n_t)])
    cot_here = lax.ppermute(
        cot,
        ("x", "yh", "yl", "z"),
        [(a * 8 + b, b * 8 + a) for a in range(8) for b in range(8)],
    )
    keep = cut(cot_rows, core * half, half, 2)
    come = flip(cut(cot_rows, (1 - core) * half, half, 2), "c")
    pre_f = narrow_preact.astype(F32)
    hid_keep = jnp.einsum("dtk,dfk->tf", keep, down_cols, preferred_element_type=F32)
    hid_send = jnp.einsum("dtk,dfk->tf", come, down_cols, preferred_element_type=F32)
    hidden_grad = hid_keep + flip(hid_send, "c")
    narrow_pre_grad = (hidden_grad * silu_slope(pre_f)).astype(BF16)

    narrow_act = jax.nn.silu(pre_f).astype(BF16)
    down_term = jnp.einsum("tf,dtk->fdk", narrow_act, cot_rows, preferred_element_type=F32)
    narrow_down_grad = lax.psum_scatter(
        down_term.astype(BF16).reshape(side, n_d * side), ("x", "yh", "c"), scatter_dimension=1, tiled=True
    )

    pre_all = gather_all(narrow_pre_grad, CHIPS, n_d).reshape(n_d * tokens, -1)
    up_other = flip(narrow_up, "c")
    up_rows = jnp.concatenate(
        [jnp.where(core == 0, narrow_up, up_other), jnp.where(core == 0, up_other, narrow_up)]
    )
    share = dot(pre_all, up_rows, ((1,), (1,))).astype(BF16)
    share = exchange(share.reshape(n_t, tokens, -1), TOK)
    own = (cot_here.astype(F32) + jnp.sum(share.astype(F32), axis=0)).astype(BF16)
    blocks = gather_all(own, CHIPS, n_d)
    rows = blocks.transpose(1, 0, 2).reshape(tokens, -1)
    rows_other = flip(rows, "c")
    boundary = jnp.concatenate(
        [jnp.where(core == 0, rows, rows_other), jnp.where(core == 0, rows_other, rows)]
    )

    wide_hidden_grad = dot(boundary, wide_down, ((1,), (1,)))
    wide_pre_grad = (wide_hidden_grad * silu_slope(wide_pre)).astype(BF16)
    input_own, input_pair = z_columns(after(wide_input, near), yl, z, core, side)
    grad_rows = z_rows(wide_pre_grad)
    up_come = flip(dot(input_pair, grad_rows, ((0,), (0,))).astype(BF16), "yl")
    wide_up_grad = (dot(input_own, grad_rows, ((0,), (0,))) + up_come.astype(F32)).astype(BF16)

    term_come = flip(term_blocks(wide_pre_grad, wide_up, 1 - core, half), "c")
    term_all = exchange(term_blocks(wide_pre_grad, wide_up, core, half, (term_come,)), CHIPS)
    own_cols = cut(boundary, (chip * 2 + core) * half, half, 1)
    wide_input_grad = (own_cols.astype(F32) + jnp.sum(term_all.astype(F32), axis=0)).astype(BF16)

    bound = exchange(after(blocks, wide_pre_grad), TOK).reshape(n_t * tokens, side)
    bound_other = flip(bound, "c")
    act_all = act_all.reshape(n_t, 2, tokens, -1)

    def act_of(parity):
        return pick(act_all, parity, 1).reshape(n_t * tokens, -1)

    wide_down_grad = (
        dot(act_of(core), bound, ((0,), (0,))) + dot(act_of(1 - core), bound_other, ((0,), (0,)))
    ).astype(BF16)

    in_blocks = after(narrow_input, pre_all).reshape(tokens, n_d, -1).transpose(1, 0, 2)
    in_near = chip_blocks(in_blocks, x, yh).reshape((4, 2, tokens, -1))
    in_own = jnp.stack(
        [pick(pick(in_near, x ^ (i // 2), 0), yh ^ (i % 2), 0) for i in range(n_d)]
    ).reshape(n_d * tokens, -1)
    up_part = dot(in_own, pre_all, ((0,), (0,)))
    up_send = cut(up_part, (1 - core) * half, half, 0).astype(BF16)
    narrow_up_grad = (cut(up_part, core * half, half, 0) + flip(up_send, "c").astype(F32)).astype(BF16)
    return (wide_input_grad, wide_up_grad, wide_down_grad, narrow_up_grad, narrow_down_grad)


def solution(mesh):
    fine = Mesh(mesh.devices.reshape(4, 2, 2, 2, 4), ("x", "yh", "c", "yl", "z"))
    dp = ("x", "yh", "c")
    tensor = ("yl", "z")
    in_specs = (
        P(None, dp),
        P(dp, None),
        P(dp, tensor),
        P(tensor, dp),
        P(tensor, None),
        P(tensor, dp),
        P(dp, None),
        P(dp, tensor),
        P(dp, tensor),
    )
    out_specs = (
        P(tensor, dp),
        P(tensor, dp),
        P(dp, tensor),
        P(dp, tensor),
        P(tensor, dp),
    )
    return jax.shard_map(body, mesh=fine, in_specs=in_specs, out_specs=out_specs, check_vma=False)
```

```python
import jax
import jax.numpy as jnp
from jax import lax
from jax.experimental import pallas as pl
from jax.experimental.pallas import tpu as pltpu
from jax.sharding import Mesh, PartitionSpec as P

BF16 = jnp.bfloat16
F32 = jnp.float32
CHIPS = ("x", "yh")
TOK = ("yl", "z")


def silu_slope(values):
    sig = jax.nn.sigmoid(values)
    return sig * (1.0 + values * (1.0 - sig))


def dot(left, right, dims):
    return lax.dot_general(left, right, (dims, ((), ())), preferred_element_type=F32)


def gate(*values):
    return lax.optimization_barrier(values)


def flip(value, axis, by=1):
    size = lax.axis_size(axis)
    return lax.ppermute(value, axis, [(i, i ^ by) for i in range(size)])


def exchange(value, axes):
    return lax.all_to_all(value, axes, 0, 0, tiled=True)


def gather_all(value, axes, count):
    return exchange(jnp.broadcast_to(value[None], (count,) + value.shape), axes)


def pick(value, index, axis):
    return lax.dynamic_index_in_dim(value, index, axis, keepdims=False)


def cut(value, start, size, axis):
    return lax.dynamic_slice_in_dim(value, start, size, axis)


def gate(*values):
    return lax.optimization_barrier(values)


def flip(value, axis, by=1):
    size = lax.axis_size(axis)
    return lax.ppermute(value, axis, [(i, i ^ by) for i in range(size)])


def exchange(value, axes):
    return lax.all_to_all(value, axes, 0, 0, tiled=True)


def gather_all(value, axes, count):
    return exchange(jnp.broadcast_to(value[None], (count,) + value.shape), axes)


def pick(value, index, axis):
    return lax.dynamic_index_in_dim(value, index, axis, keepdims=False)


def cut(value, start, size, axis):
    return lax.dynamic_slice_in_dim(value, start, size, axis)


def after(value, *others):
    return lax.optimization_barrier((value,) + others)[0]


def z_rows(block):
    return jnp.concatenate([block] + [flip(block, "z", by) for by in (1, 2, 3)])


def term_kernel(core_ref, grad_ref, up_ref, keep_ref, send_ref):
    half = keep_ref.shape[2]
    part = lax.dot_general(
        grad_ref[...], up_ref[...], (((1,), (1,)), ((), ())), preferred_element_type=F32
    )
    first, second = part[:, :half], part[:, half:]
    even = core_ref[0] == 0
    keep_ref[0] = jnp.where(even, first, second)
    send_ref[0] = jnp.where(even, second, first).astype(BF16)


def term_blocks(grad, up, core, half):
    rows, depth = grad.shape
    count = up.shape[0] // (2 * half)
    block = pl.BlockSpec((1, rows, half), lambda i, core: (i, 0, 0))
    shape = (count, rows, half)
    return pl.pallas_call(
        term_kernel,
        grid_spec=pltpu.PrefetchScalarGridSpec(
            num_scalar_prefetch=1,
            grid=(count,),
            in_specs=[
                pl.BlockSpec((rows, depth), lambda i, core: (0, 0)),
                pl.BlockSpec((2 * half, depth), lambda i, core: (i, 0)),
            ],
            out_specs=[block, block],
        ),
        out_shape=[jax.ShapeDtypeStruct(shape, F32), jax.ShapeDtypeStruct(shape, BF16)],
        cost_estimate=pl.CostEstimate(
            flops=4 * count * rows * half * depth,
            bytes_accessed=4 * count * half * depth,
            transcendentals=0,
        ),
        compiler_params=pltpu.CompilerParams(vmem_limit_bytes=20 * 1024 * 1024),
        name="term",
    )(core.reshape(1).astype(jnp.int32), grad, up)


def body(
    wide_up,
    wide_down,
    narrow_up,
    narrow_down,
    wide_input,
    wide_preact,
    narrow_input,
    narrow_preact,
    cotangent,
):
    core = lax.axis_index("c")
    z = lax.axis_index("z")
    yl = lax.axis_index("yl")
    x = lax.axis_index("x")
    yh = lax.axis_index("yh")
    chip = x * 2 + yh
    tokens, side = cotangent.shape
    n_t, n_d = 8, 8
    half = narrow_down.shape[1]

    wide_pre = wide_preact.astype(F32)
    wide_act = jax.nn.silu(wide_pre).astype(BF16)
    act_all = lax.all_gather(wide_act, TOK, axis=0, tiled=True)

    down_come = flip(narrow_down, "yh")
    down_come, up_mine, cot = gate(down_come, narrow_up, cotangent)
    down_pair = jnp.stack([narrow_down, down_come])
    down_cols = jnp.concatenate([down_pair] + [flip(down_pair, "x", by) for by in (1, 2, 3)])
    up_other, cot = gate(flip(up_mine, "c"), cot)
    cot_rows = gather_all(cot, TOK, n_t)
    cot_near = jnp.stack(
        [pick(cot_rows, (x ^ k) * 2 + (yh ^ r), 0) for k in range(4) for r in range(2)]
    )
    keep = cut(cot_near, core * half, half, 2)
    come = flip(cut(cot_near, (1 - core) * half, half, 2), "c")
    down_cols, come, keep = gate(down_cols, come, keep)

    pre_f = narrow_preact.astype(F32)
    hid_send = jnp.einsum("dtk,dfk->tf", come, down_cols, preferred_element_type=F32)
    hid_keep = jnp.einsum("dtk,dfk->tf", keep, down_cols, preferred_element_type=F32)
    hidden_grad = hid_keep + flip(hid_send, "c")
    narrow_pre_grad = (hidden_grad * silu_slope(pre_f)).astype(BF16)

    pre_copies = jnp.broadcast_to(narrow_pre_grad[None], (n_d, tokens, side))
    pre_copies, turned, source = gate(pre_copies, cotangent, wide_input)
    pre_all = exchange(pre_copies, CHIPS).reshape(n_d * tokens, -1)
    group = jnp.where(core == 0, yl, 1 - yl)
    got = [flip(cut(source, (group * 4 + (z ^ by)) * side, side, 1), "z", by) for by in (1, 2, 3)]
    turned = lax.ppermute(
        turned, ("x", "yh", "yl", "z"), [(a * 8 + b, b * 8 + a) for a in range(8) for b in range(8)]
    )
    up_rows = jnp.concatenate(
        [jnp.where(core == 0, narrow_up, up_other), jnp.where(core == 0, up_other, narrow_up)]
    )
    narrow_act = jax.nn.silu(pre_f).astype(BF16)
    down_term = dot(narrow_act, cot_rows.transpose(1, 0, 2).reshape(tokens, -1), ((0,), (0,)))
    pre_all, up_rows, got, turned, down_term = gate(
        pre_all, up_rows, tuple(got), turned, down_term.astype(BF16)
    )
    narrow_down_grad = lax.psum_scatter(
        down_term, ("x", "yh", "c"), scatter_dimension=1, tiled=True
    )

    share = dot(pre_all, up_rows, ((1,), (1,))).astype(BF16)
    share, got = gate(share, jnp.concatenate(got))
    other = flip(got, "c")
    share = exchange(share.reshape(n_t, tokens, -1), TOK)
    share, other, act_all = gate(share, other, act_all)
    own = (turned.astype(F32) + jnp.sum(share.astype(F32), axis=0)).astype(BF16)
    blocks = gather_all(own, CHIPS, n_d)
    mine = cut(wide_input, (yl * 4 + z) * side, side, 1)
    pair = cut(wide_input, ((1 - yl) * 4 + z) * side, side, 1)
    input_own = jnp.concatenate([mine, jnp.where(core == 0, got, other)])
    input_pair = jnp.concatenate([pair, jnp.where(core == 0, other, got)])
    in_blocks = narrow_input.reshape(tokens, n_d, -1).transpose(1, 0, 2)
    blocks, input_pair, input_own, in_blocks = gate(blocks, input_pair, input_own, in_blocks)
    rows = blocks.transpose(1, 0, 2).reshape(tokens, -1)
    rows, blocks = gate(rows, blocks)
    rows_other = flip(rows, "c")
    boundary = jnp.concatenate(
        [jnp.where(core == 0, rows, rows_other), jnp.where(core == 0, rows_other, rows)]
    )
    bound = exchange(blocks, TOK)

    wide_hidden_grad = dot(boundary, wide_down, ((1,), (1,)))
    wide_pre_grad = (wide_hidden_grad * silu_slope(wide_pre)).astype(BF16)
    grad_rows = z_rows(wide_pre_grad)
    term_keep, term_send = term_blocks(wide_pre_grad, wide_up, core, half)
    term_send, in_blocks = gate(term_send, in_blocks)
    term_chip = (term_keep + flip(term_send, "c").astype(F32)).astype(BF16)
    in_own = exchange(in_blocks, CHIPS).reshape(n_d * tokens, side)
    term_chip, bound_other, in_own = gate(term_chip, flip(bound, "c"), in_own)
    term_all = exchange(term_chip, CHIPS)

    up_send = dot(input_pair, grad_rows, ((0,), (0,))).astype(BF16)
    up_come = flip(up_send, "yl")

    bound = jnp.stack(
        [jnp.where(core == 0, bound, bound_other), jnp.where(core == 0, bound_other, bound)], axis=1
    ).reshape(-1, side)
    wide_down_grad = dot(act_all, bound, ((0,), (0,))).astype(BF16)

    up_part = dot(in_own, pre_all, ((0,), (0,)))
    narrow_send = cut(up_part, (1 - core) * half, half, 0).astype(BF16)
    narrow_keep = cut(up_part, core * half, half, 0)
    narrow_up_grad = (narrow_keep + flip(narrow_send, "c").astype(F32)).astype(BF16)

    up_come, wide_down_grad, narrow_up_grad = gate(up_come, wide_down_grad, narrow_up_grad)
    wide_up_grad = (dot(input_own, grad_rows, ((0,), (0,))) + up_come.astype(F32)).astype(BF16)
    own_cols = cut(boundary, (chip * 2 + core) * half, half, 1)
    wide_input_grad = (own_cols.astype(F32) + jnp.sum(term_all.astype(F32), axis=0)).astype(BF16)
    return (wide_input_grad, wide_up_grad, wide_down_grad, narrow_up_grad, narrow_down_grad)


def solution(mesh):
    fine = Mesh(mesh.devices.reshape(4, 2, 2, 2, 4), ("x", "yh", "c", "yl", "z"))
    dp = ("x", "yh", "c")
    tensor = ("yl", "z")
    in_specs = (
        P(None, dp),
        P(dp, None),
        P(dp, tensor),
        P(tensor, dp),
        P(tensor, None),
        P(tensor, dp),
        P(dp, None),
        P(dp, tensor),
        P(dp, tensor),
    )
    out_specs = (
        P(tensor, dp),
        P(tensor, dp),
        P(dp, tensor),
        P(dp, tensor),
        P(tensor, dp),
    )
    return jax.shard_map(body, mesh=fine, in_specs=in_specs, out_specs=out_specs, check_vma=False)
```

```python
import jax
import jax.numpy as jnp
from jax import lax
from jax.experimental import pallas as pl
from jax.experimental.pallas import tpu as pltpu
from jax.sharding import Mesh, PartitionSpec as P

BF16 = jnp.bfloat16
F32 = jnp.float32
CHIPS = ("x", "yh")
TOK = ("yl", "z")


def silu_slope(values):
    sig = jax.nn.sigmoid(values)
    return sig * (1.0 + values * (1.0 - sig))


def dot(left, right, dims):
    return lax.dot_general(left, right, (dims, ((), ())), preferred_element_type=F32)


def gate(*values):
    return lax.optimization_barrier(values)


def flip(value, axis, by=1):
    size = lax.axis_size(axis)
    return lax.ppermute(value, axis, [(i, i ^ by) for i in range(size)])


def exchange(value, axes):
    return lax.all_to_all(value, axes, 0, 0, tiled=True)


def gather_all(value, axes, count):
    return exchange(jnp.broadcast_to(value[None], (count,) + value.shape), axes)


def pick(value, index, axis):
    return lax.dynamic_index_in_dim(value, index, axis, keepdims=False)


def cut(value, start, size, axis):
    return lax.dynamic_slice_in_dim(value, start, size, axis)


def gate(*values):
    return lax.optimization_barrier(values)


def flip(value, axis, by=1):
    size = lax.axis_size(axis)
    return lax.ppermute(value, axis, [(i, i ^ by) for i in range(size)])


def exchange(value, axes):
    return lax.all_to_all(value, axes, 0, 0, tiled=True)


def gather_all(value, axes, count):
    return exchange(jnp.broadcast_to(value[None], (count,) + value.shape), axes)


def pick(value, index, axis):
    return lax.dynamic_index_in_dim(value, index, axis, keepdims=False)


def cut(value, start, size, axis):
    return lax.dynamic_slice_in_dim(value, start, size, axis)


def after(value, *others):
    return lax.optimization_barrier((value,) + others)[0]


def z_rows(block):
    return jnp.concatenate([block] + [flip(block, "z", by) for by in (1, 2, 3)])


def term_kernel(core_ref, grad_ref, up_ref, keep_ref, send_ref):
    half = keep_ref.shape[2]
    part = lax.dot_general(
        grad_ref[...], up_ref[...], (((1,), (1,)), ((), ())), preferred_element_type=F32
    )
    first, second = part[:, :half], part[:, half:]
    even = core_ref[0] == 0
    keep_ref[0] = jnp.where(even, first, second)
    send_ref[0] = jnp.where(even, second, first).astype(BF16)


def term_blocks(grad, up, core, half):
    rows, depth = grad.shape
    count = up.shape[0] // (2 * half)
    block = pl.BlockSpec((1, rows, half), lambda i, core: (i, 0, 0))
    shape = (count, rows, half)
    return pl.pallas_call(
        term_kernel,
        grid_spec=pltpu.PrefetchScalarGridSpec(
            num_scalar_prefetch=1,
            grid=(count,),
            in_specs=[
                pl.BlockSpec((rows, depth), lambda i, core: (0, 0)),
                pl.BlockSpec((2 * half, depth), lambda i, core: (i, 0)),
            ],
            out_specs=[block, block],
        ),
        out_shape=[jax.ShapeDtypeStruct(shape, F32), jax.ShapeDtypeStruct(shape, BF16)],
        cost_estimate=pl.CostEstimate(
            flops=4 * count * rows * half * depth,
            bytes_accessed=4 * count * half * depth,
            transcendentals=0,
        ),
        compiler_params=pltpu.CompilerParams(vmem_limit_bytes=20 * 1024 * 1024),
        name="term",
    )(core.reshape(1).astype(jnp.int32), grad, up)


def body(
    wide_up,
    wide_down,
    narrow_up,
    narrow_down,
    wide_input,
    wide_preact,
    narrow_input,
    narrow_preact,
    cotangent,
):
    core = lax.axis_index("c")
    z = lax.axis_index("z")
    yl = lax.axis_index("yl")
    x = lax.axis_index("x")
    yh = lax.axis_index("yh")
    chip = x * 2 + yh
    tokens, side = cotangent.shape
    n_t, n_d = 8, 8
    half = narrow_down.shape[1]

    wide_pre = wide_preact.astype(F32)
    wide_act = jax.nn.silu(wide_pre).astype(BF16)
    act_all = lax.all_gather(wide_act, TOK, axis=0, tiled=True)

    down_come = flip(narrow_down, "yh")
    down_come, up_mine, cot = gate(down_come, narrow_up, cotangent)
    down_pair = jnp.stack([narrow_down, down_come])
    down_cols = jnp.concatenate([down_pair] + [flip(down_pair, "x", by) for by in (1, 2, 3)])
    up_other, cot = gate(flip(up_mine, "c"), cot)
    cot_rows = gather_all(cot, TOK, n_t)
    cot_near = jnp.stack(
        [pick(cot_rows, (x ^ k) * 2 + (yh ^ r), 0) for k in range(4) for r in range(2)]
    )
    keep = cut(cot_near, core * half, half, 2)
    come = flip(cut(cot_near, (1 - core) * half, half, 2), "c")
    down_cols, come, keep = gate(down_cols, come, keep)

    pre_f = narrow_preact.astype(F32)
    hid_send = jnp.einsum("dtk,dfk->tf", come, down_cols, preferred_element_type=F32)
    hid_keep = jnp.einsum("dtk,dfk->tf", keep, down_cols, preferred_element_type=F32)
    hidden_grad = hid_keep + flip(hid_send, "c")
    narrow_pre_grad = (hidden_grad * silu_slope(pre_f)).astype(BF16)

    pre_copies = jnp.broadcast_to(narrow_pre_grad[None], (n_d, tokens, side))
    pre_copies, turned = gate(pre_copies, cotangent)
    pre_all = exchange(pre_copies, CHIPS).reshape(n_d * tokens, -1)
    turned = lax.ppermute(
        turned, ("x", "yh", "yl", "z"), [(a * 8 + b, b * 8 + a) for a in range(8) for b in range(8)]
    )
    up_rows = jnp.concatenate(
        [jnp.where(core == 0, narrow_up, up_other), jnp.where(core == 0, up_other, narrow_up)]
    )
    narrow_act = jax.nn.silu(pre_f).astype(BF16)
    down_term = dot(narrow_act, cot_rows.transpose(1, 0, 2).reshape(tokens, -1), ((0,), (0,)))
    pre_all, up_rows, turned, down_term, act_all = gate(
        pre_all, up_rows, turned, down_term.astype(BF16), act_all
    )
    narrow_down_grad = lax.psum_scatter(
        down_term, ("x", "yh", "c"), scatter_dimension=1, tiled=True
    )

    share = dot(pre_all, up_rows, ((1,), (1,))).astype(BF16)
    share = exchange(share.reshape(n_t, tokens, -1), TOK)
    own = (turned.astype(F32) + jnp.sum(share.astype(F32), axis=0)).astype(BF16)
    own_copies = jnp.broadcast_to(own[None], (n_d, tokens, side))
    own_copies, source = gate(own_copies, wide_input)
    blocks = exchange(own_copies, CHIPS)
    group = jnp.where(core == 0, yl, 1 - yl)
    got = [flip(cut(source, (group * 4 + (z ^ by)) * side, side, 1), "z", by) for by in (1, 2, 3)]
    in_blocks = narrow_input.reshape(tokens, n_d, -1).transpose(1, 0, 2)
    blocks, got, in_blocks = gate(blocks, tuple(got), in_blocks)
    got = jnp.concatenate(got)
    rows = blocks.transpose(1, 0, 2).reshape(tokens, -1)
    rows, blocks = gate(rows, blocks)
    rows_other = flip(rows, "c")
    boundary = jnp.concatenate(
        [jnp.where(core == 0, rows, rows_other), jnp.where(core == 0, rows_other, rows)]
    )
    bound = exchange(blocks, TOK)

    wide_hidden_grad = dot(boundary, wide_down, ((1,), (1,)))
    wide_pre_grad = (wide_hidden_grad * silu_slope(wide_pre)).astype(BF16)
    wide_pre_grad, got = gate(wide_pre_grad, got)
    grad_rows = z_rows(wide_pre_grad)
    term_keep, term_send = term_blocks(wide_pre_grad, wide_up, core, half)
    term_send, in_blocks = gate(term_send, in_blocks)
    term_chip = (term_keep + flip(term_send, "c").astype(F32)).astype(BF16)
    in_own = exchange(in_blocks, CHIPS).reshape(n_d * tokens, side)
    term_chip, bound_other, narrow_down_grad = gate(term_chip, flip(bound, "c"), narrow_down_grad)
    term_all = exchange(term_chip, CHIPS)

    other = flip(got, "c")
    mine = cut(wide_input, (yl * 4 + z) * side, side, 1)
    pair = cut(wide_input, ((1 - yl) * 4 + z) * side, side, 1)
    input_own = jnp.concatenate([mine, jnp.where(core == 0, got, other)])
    input_pair = jnp.concatenate([pair, jnp.where(core == 0, other, got)])
    up_send = dot(input_pair, grad_rows, ((0,), (0,))).astype(BF16)
    up_come = flip(up_send, "yl")

    bound = jnp.stack(
        [jnp.where(core == 0, bound, bound_other), jnp.where(core == 0, bound_other, bound)], axis=1
    ).reshape(-1, side)
    wide_down_grad = dot(act_all, bound, ((0,), (0,))).astype(BF16)

    wide_down_grad, in_own = gate(wide_down_grad, in_own)
    up_part = dot(in_own, pre_all, ((0,), (0,)))
    narrow_send = cut(up_part, (1 - core) * half, half, 0).astype(BF16)
    narrow_keep = cut(up_part, core * half, half, 0)
    narrow_up_grad = (narrow_keep + flip(narrow_send, "c").astype(F32)).astype(BF16)

    up_come, wide_down_grad, narrow_up_grad = gate(up_come, wide_down_grad, narrow_up_grad)
    wide_up_grad = (dot(input_own, grad_rows, ((0,), (0,))) + up_come.astype(F32)).astype(BF16)
    own_cols = cut(boundary, (chip * 2 + core) * half, half, 1)
    wide_up_grad, own_cols = gate(wide_up_grad, own_cols)
    wide_input_grad = (own_cols.astype(F32) + jnp.sum(term_all.astype(F32), axis=0)).astype(BF16)
    return (wide_input_grad, wide_up_grad, wide_down_grad, narrow_up_grad, narrow_down_grad)


def solution(mesh):
    fine = Mesh(mesh.devices.reshape(4, 2, 2, 2, 4), ("x", "yh", "c", "yl", "z"))
    dp = ("x", "yh", "c")
    tensor = ("yl", "z")
    in_specs = (
        P(None, dp),
        P(dp, None),
        P(dp, tensor),
        P(tensor, dp),
        P(tensor, None),
        P(tensor, dp),
        P(dp, None),
        P(dp, tensor),
        P(dp, tensor),
    )
    out_specs = (
        P(tensor, dp),
        P(tensor, dp),
        P(dp, tensor),
        P(dp, tensor),
        P(tensor, dp),
    )
    return jax.shard_map(body, mesh=fine, in_specs=in_specs, out_specs=out_specs, check_vma=False)
```

```python
import jax
import jax.numpy as jnp
from jax import lax
from jax.experimental import pallas as pl
from jax.experimental.pallas import tpu as pltpu
from jax.sharding import Mesh, PartitionSpec as P

BF16 = jnp.bfloat16
F32 = jnp.float32
CHIPS = ("x", "yh")
TOK = ("yl", "z")


def silu_slope(values):
    sig = jax.nn.sigmoid(values)
    return sig * (1.0 + values * (1.0 - sig))


def dot(left, right, dims):
    return lax.dot_general(left, right, (dims, ((), ())), preferred_element_type=F32)


def gate(*values):
    return lax.optimization_barrier(values)


def flip(value, axis, by=1):
    size = lax.axis_size(axis)
    return lax.ppermute(value, axis, [(i, i ^ by) for i in range(size)])


def exchange(value, axes):
    return lax.all_to_all(value, axes, 0, 0, tiled=True)


def gather_all(value, axes, count):
    return exchange(jnp.broadcast_to(value[None], (count,) + value.shape), axes)


def pick(value, index, axis):
    return lax.dynamic_index_in_dim(value, index, axis, keepdims=False)


def cut(value, start, size, axis):
    return lax.dynamic_slice_in_dim(value, start, size, axis)


def gate(*values):
    return lax.optimization_barrier(values)


def flip(value, axis, by=1):
    size = lax.axis_size(axis)
    return lax.ppermute(value, axis, [(i, i ^ by) for i in range(size)])


def exchange(value, axes):
    return lax.all_to_all(value, axes, 0, 0, tiled=True)


def gather_all(value, axes, count):
    return exchange(jnp.broadcast_to(value[None], (count,) + value.shape), axes)


def pick(value, index, axis):
    return lax.dynamic_index_in_dim(value, index, axis, keepdims=False)


def cut(value, start, size, axis):
    return lax.dynamic_slice_in_dim(value, start, size, axis)


def after(value, *others):
    return lax.optimization_barrier((value,) + others)[0]


def z_rows(block):
    return jnp.concatenate([block] + [flip(block, "z", by) for by in (1, 2, 3)])


def term_kernel(core_ref, grad_ref, up_ref, keep_ref, send_ref):
    half = keep_ref.shape[2]
    part = lax.dot_general(
        grad_ref[...], up_ref[...], (((1,), (1,)), ((), ())), preferred_element_type=F32
    )
    first, second = part[:, :half], part[:, half:]
    even = core_ref[0] == 0
    keep_ref[0] = jnp.where(even, first, second)
    send_ref[0] = jnp.where(even, second, first).astype(BF16)


def term_blocks(grad, up, core, half):
    rows, depth = grad.shape
    count = up.shape[0] // (2 * half)
    block = pl.BlockSpec((1, rows, half), lambda i, core: (i, 0, 0))
    shape = (count, rows, half)
    return pl.pallas_call(
        term_kernel,
        grid_spec=pltpu.PrefetchScalarGridSpec(
            num_scalar_prefetch=1,
            grid=(count,),
            in_specs=[
                pl.BlockSpec((rows, depth), lambda i, core: (0, 0)),
                pl.BlockSpec((2 * half, depth), lambda i, core: (i, 0)),
            ],
            out_specs=[block, block],
        ),
        out_shape=[jax.ShapeDtypeStruct(shape, F32), jax.ShapeDtypeStruct(shape, BF16)],
        cost_estimate=pl.CostEstimate(
            flops=4 * count * rows * half * depth,
            bytes_accessed=4 * count * half * depth,
            transcendentals=0,
        ),
        compiler_params=pltpu.CompilerParams(vmem_limit_bytes=20 * 1024 * 1024),
        name="term",
    )(core.reshape(1).astype(jnp.int32), grad, up)


def body(
    wide_up,
    wide_down,
    narrow_up,
    narrow_down,
    wide_input,
    wide_preact,
    narrow_input,
    narrow_preact,
    cotangent,
):
    core = lax.axis_index("c")
    z = lax.axis_index("z")
    yl = lax.axis_index("yl")
    x = lax.axis_index("x")
    yh = lax.axis_index("yh")
    chip = x * 2 + yh
    tokens, side = cotangent.shape
    n_t, n_d = 8, 8
    half = narrow_down.shape[1]

    wide_pre = wide_preact.astype(F32)
    wide_act = jax.nn.silu(wide_pre).astype(BF16)
    act_all = lax.all_gather(wide_act, TOK, axis=0, tiled=True)

    down_come = flip(narrow_down, "yh")
    down_come, up_mine, cot = gate(down_come, narrow_up, cotangent)
    down_pair = jnp.stack([narrow_down, down_come])
    down_cols = jnp.concatenate([down_pair] + [flip(down_pair, "x", by) for by in (1, 2, 3)])
    up_other = flip(up_mine, "c")
    cot_rows = gather_all(cot, TOK, n_t)
    cot_near = jnp.stack(
        [pick(cot_rows, (x ^ k) * 2 + (yh ^ r), 0) for k in range(4) for r in range(2)]
    )
    keep = cut(cot_near, core * half, half, 2)
    come = flip(cut(cot_near, (1 - core) * half, half, 2), "c")
    down_cols, come, keep, up_other = gate(down_cols, come, keep, up_other)

    pre_f = narrow_preact.astype(F32)
    hid_send = jnp.einsum("dtk,dfk->tf", come, down_cols, preferred_element_type=F32)
    hid_keep = jnp.einsum("dtk,dfk->tf", keep, down_cols, preferred_element_type=F32)
    hidden_grad = hid_keep + flip(hid_send, "c")
    narrow_pre_grad = (hidden_grad * silu_slope(pre_f)).astype(BF16)

    pre_copies = jnp.broadcast_to(narrow_pre_grad[None], (n_d, tokens, side))
    pre_copies, turned = gate(pre_copies, cotangent)
    pre_all = exchange(pre_copies, CHIPS).reshape(n_d * tokens, -1)
    turned = lax.ppermute(
        turned, ("x", "yh", "yl", "z"), [(a * 8 + b, b * 8 + a) for a in range(8) for b in range(8)]
    )
    up_rows = jnp.concatenate(
        [jnp.where(core == 0, narrow_up, up_other), jnp.where(core == 0, up_other, narrow_up)]
    )
    narrow_act = jax.nn.silu(pre_f).astype(BF16)
    down_term = dot(narrow_act, cot_rows.transpose(1, 0, 2).reshape(tokens, -1), ((0,), (0,)))
    pre_all, up_rows, turned, down_term, act_all = gate(
        pre_all, up_rows, turned, down_term.astype(BF16), act_all
    )
    narrow_down_grad = lax.psum_scatter(
        down_term, ("x", "yh", "c"), scatter_dimension=1, tiled=True
    )

    share = dot(pre_all, up_rows, ((1,), (1,))).astype(BF16)
    share = exchange(share.reshape(n_t, tokens, -1), TOK)
    own = (turned.astype(F32) + jnp.sum(share.astype(F32), axis=0)).astype(BF16)
    own_copies = jnp.broadcast_to(own[None], (n_d, tokens, side))
    own_copies, source = gate(own_copies, wide_input)
    blocks = exchange(own_copies, CHIPS)
    group = jnp.where(core == 0, yl, 1 - yl)
    got = [flip(cut(source, (group * 4 + (z ^ by)) * side, side, 1), "z", by) for by in (1, 2, 3)]
    in_blocks = narrow_input.reshape(tokens, n_d, -1).transpose(1, 0, 2)
    blocks, got, in_blocks = gate(blocks, tuple(got), in_blocks)
    got = jnp.concatenate(got)
    rows = blocks.transpose(1, 0, 2).reshape(tokens, -1)
    rows, blocks = gate(rows, blocks)
    rows_other = flip(rows, "c")
    boundary = jnp.concatenate(
        [jnp.where(core == 0, rows, rows_other), jnp.where(core == 0, rows_other, rows)]
    )
    bound = exchange(blocks, TOK)

    wide_hidden_grad = dot(boundary, wide_down, ((1,), (1,)))
    wide_pre_grad = (wide_hidden_grad * silu_slope(wide_pre)).astype(BF16)
    wide_pre_grad, got = gate(wide_pre_grad, got)
    grad_rows = z_rows(wide_pre_grad)
    term_keep, term_send = term_blocks(wide_pre_grad, wide_up, core, half)
    term_send, in_blocks = gate(term_send, in_blocks)
    term_chip = (term_keep + flip(term_send, "c").astype(F32)).astype(BF16)
    in_own = exchange(in_blocks, CHIPS).reshape(n_d * tokens, side)
    term_chip, bound_other, narrow_down_grad = gate(term_chip, flip(bound, "c"), narrow_down_grad)
    term_all = exchange(term_chip, CHIPS)

    other = flip(got, "c")
    mine = cut(wide_input, (yl * 4 + z) * side, side, 1)
    pair = cut(wide_input, ((1 - yl) * 4 + z) * side, side, 1)
    input_own = jnp.concatenate([mine, jnp.where(core == 0, got, other)])
    input_pair = jnp.concatenate([pair, jnp.where(core == 0, other, got)])
    up_send = dot(input_pair, grad_rows, ((0,), (0,))).astype(BF16)
    up_come = flip(up_send, "yl")

    bound = jnp.stack(
        [jnp.where(core == 0, bound, bound_other), jnp.where(core == 0, bound_other, bound)], axis=1
    ).reshape(-1, side)
    wide_down_grad = dot(act_all, bound, ((0,), (0,))).astype(BF16)

    wide_down_grad, in_own = gate(wide_down_grad, in_own)
    up_part = dot(in_own, pre_all, ((0,), (0,)))
    narrow_send = cut(up_part, (1 - core) * half, half, 0).astype(BF16)
    narrow_keep = cut(up_part, core * half, half, 0)
    narrow_up_grad = (narrow_keep + flip(narrow_send, "c").astype(F32)).astype(BF16)

    up_come, wide_down_grad, narrow_up_grad = gate(up_come, wide_down_grad, narrow_up_grad)
    wide_up_grad = (dot(input_own, grad_rows, ((0,), (0,))) + up_come.astype(F32)).astype(BF16)
    own_cols = cut(boundary, (chip * 2 + core) * half, half, 1)
    wide_up_grad, own_cols = gate(wide_up_grad, own_cols)
    wide_input_grad = (own_cols.astype(F32) + jnp.sum(term_all.astype(F32), axis=0)).astype(BF16)
    return (wide_input_grad, wide_up_grad, wide_down_grad, narrow_up_grad, narrow_down_grad)


def solution(mesh):
    fine = Mesh(mesh.devices.reshape(4, 2, 2, 2, 4), ("x", "yh", "c", "yl", "z"))
    dp = ("x", "yh", "c")
    tensor = ("yl", "z")
    in_specs = (
        P(None, dp),
        P(dp, None),
        P(dp, tensor),
        P(tensor, dp),
        P(tensor, None),
        P(tensor, dp),
        P(dp, None),
        P(dp, tensor),
        P(dp, tensor),
    )
    out_specs = (
        P(tensor, dp),
        P(tensor, dp),
        P(dp, tensor),
        P(dp, tensor),
        P(tensor, dp),
    )
    return jax.shard_map(body, mesh=fine, in_specs=in_specs, out_specs=out_specs, check_vma=False)
```

```python
import jax
import jax.numpy as jnp
from jax import lax
from jax.experimental import pallas as pl
from jax.experimental.pallas import tpu as pltpu
from jax.sharding import Mesh, PartitionSpec as P

BF16 = jnp.bfloat16
F32 = jnp.float32
CHIPS = ("x", "yh")
TOK = ("yl", "z")


def silu_slope(values):
    sig = jax.nn.sigmoid(values)
    return sig * (1.0 + values * (1.0 - sig))


def dot(left, right, dims):
    return lax.dot_general(left, right, (dims, ((), ())), preferred_element_type=F32)


def gate(*values):
    return lax.optimization_barrier(values)


def flip(value, axis, by=1):
    size = lax.axis_size(axis)
    return lax.ppermute(value, axis, [(i, i ^ by) for i in range(size)])


def exchange(value, axes):
    return lax.all_to_all(value, axes, 0, 0, tiled=True)


def gather_all(value, axes, count):
    return exchange(jnp.broadcast_to(value[None], (count,) + value.shape), axes)


def pick(value, index, axis):
    return lax.dynamic_index_in_dim(value, index, axis, keepdims=False)


def cut(value, start, size, axis):
    return lax.dynamic_slice_in_dim(value, start, size, axis)


def gate(*values):
    return lax.optimization_barrier(values)


def flip(value, axis, by=1):
    size = lax.axis_size(axis)
    return lax.ppermute(value, axis, [(i, i ^ by) for i in range(size)])


def exchange(value, axes):
    return lax.all_to_all(value, axes, 0, 0, tiled=True)


def gather_all(value, axes, count):
    return exchange(jnp.broadcast_to(value[None], (count,) + value.shape), axes)


def pick(value, index, axis):
    return lax.dynamic_index_in_dim(value, index, axis, keepdims=False)


def cut(value, start, size, axis):
    return lax.dynamic_slice_in_dim(value, start, size, axis)


def after(value, *others):
    return lax.optimization_barrier((value,) + others)[0]


def z_rows(block):
    return jnp.concatenate([block] + [flip(block, "z", by) for by in (1, 2, 3)])


def term_kernel(core_ref, grad_ref, up_ref, keep_ref, send_ref):
    half = keep_ref.shape[2]
    part = lax.dot_general(
        grad_ref[...], up_ref[...], (((1,), (1,)), ((), ())), preferred_element_type=F32
    )
    first, second = part[:, :half], part[:, half:]
    even = core_ref[0] == 0
    keep_ref[0] = jnp.where(even, first, second).astype(BF16)
    send_ref[0] = jnp.where(even, second, first).astype(BF16)


def term_blocks(grad, up, core, half):
    rows, depth = grad.shape
    count = up.shape[0] // (2 * half)
    block = pl.BlockSpec((1, rows, half), lambda i, core: (i, 0, 0))
    shape = (count, rows, half)
    return pl.pallas_call(
        term_kernel,
        grid_spec=pltpu.PrefetchScalarGridSpec(
            num_scalar_prefetch=1,
            grid=(count,),
            in_specs=[
                pl.BlockSpec((rows, depth), lambda i, core: (0, 0)),
                pl.BlockSpec((2 * half, depth), lambda i, core: (i, 0)),
            ],
            out_specs=[block, block],
        ),
        out_shape=[jax.ShapeDtypeStruct(shape, BF16)] * 2,
        cost_estimate=pl.CostEstimate(
            flops=4 * count * rows * half * depth,
            bytes_accessed=4 * count * half * depth,
            transcendentals=0,
        ),
        compiler_params=pltpu.CompilerParams(vmem_limit_bytes=20 * 1024 * 1024),
        name="term",
    )(core.reshape(1).astype(jnp.int32), grad, up)


def body(
    wide_up,
    wide_down,
    narrow_up,
    narrow_down,
    wide_input,
    wide_preact,
    narrow_input,
    narrow_preact,
    cotangent,
):
    core = lax.axis_index("c")
    z = lax.axis_index("z")
    yl = lax.axis_index("yl")
    x = lax.axis_index("x")
    yh = lax.axis_index("yh")
    chip = x * 2 + yh
    tokens, side = cotangent.shape
    n_t, n_d = 8, 8
    half = narrow_down.shape[1]

    wide_pre = wide_preact.astype(F32)
    wide_act = jax.nn.silu(wide_pre).astype(BF16)
    act_all = lax.all_gather(wide_act, TOK, axis=0, tiled=True)

    down_come = flip(narrow_down, "yh")
    down_come, up_mine, cot = gate(down_come, narrow_up, cotangent)
    down_pair = jnp.stack([narrow_down, down_come])
    down_cols = jnp.concatenate([down_pair] + [flip(down_pair, "x", by) for by in (1, 2, 3)])
    up_other = flip(up_mine, "c")
    cot_rows = gather_all(cot, TOK, n_t)
    cot_near = jnp.stack(
        [pick(cot_rows, (x ^ k) * 2 + (yh ^ r), 0) for k in range(4) for r in range(2)]
    )
    keep = cut(cot_near, core * half, half, 2)
    come = flip(cut(cot_near, (1 - core) * half, half, 2), "c")
    down_cols, come, keep, up_other = gate(down_cols, come, keep, up_other)

    pre_f = narrow_preact.astype(F32)
    hid_send = jnp.einsum("dtk,dfk->tf", come, down_cols, preferred_element_type=F32)
    hid_keep = jnp.einsum("dtk,dfk->tf", keep, down_cols, preferred_element_type=F32)
    hidden_grad = hid_keep + flip(hid_send, "c")
    narrow_pre_grad = (hidden_grad * silu_slope(pre_f)).astype(BF16)

    pre_copies = jnp.broadcast_to(narrow_pre_grad[None], (n_d, tokens, side))
    pre_copies, turned = gate(pre_copies, cotangent)
    pre_all = exchange(pre_copies, CHIPS).reshape(n_d * tokens, -1)
    turned = lax.ppermute(
        turned, ("x", "yh", "yl", "z"), [(a * 8 + b, b * 8 + a) for a in range(8) for b in range(8)]
    )
    up_rows = jnp.concatenate(
        [jnp.where(core == 0, narrow_up, up_other), jnp.where(core == 0, up_other, narrow_up)]
    )
    narrow_act = jax.nn.silu(pre_f).astype(BF16)
    down_term = dot(narrow_act, cot_rows.transpose(1, 0, 2).reshape(tokens, -1), ((0,), (0,)))
    pre_all, up_rows, turned, down_term, act_all = gate(
        pre_all, up_rows, turned, down_term.astype(BF16), act_all
    )
    narrow_down_grad = lax.psum_scatter(
        down_term, ("x", "yh", "c"), scatter_dimension=1, tiled=True
    )

    share = dot(pre_all, up_rows, ((1,), (1,))).astype(BF16)
    share = exchange(share.reshape(n_t, tokens, -1), TOK)
    own = (turned.astype(F32) + jnp.sum(share.astype(F32), axis=0)).astype(BF16)
    own_copies = jnp.broadcast_to(own[None], (n_d, tokens, side))
    own_copies, source = gate(own_copies, wide_input)
    blocks = exchange(own_copies, CHIPS)
    group = jnp.where(core == 0, yl, 1 - yl)
    got = [flip(cut(source, (group * 4 + (z ^ by)) * side, side, 1), "z", by) for by in (1, 2, 3)]
    in_blocks = narrow_input.reshape(tokens, n_d, -1).transpose(1, 0, 2)
    blocks, got, in_blocks = gate(blocks, tuple(got), in_blocks)
    got = jnp.concatenate(got)
    rows = blocks.transpose(1, 0, 2).reshape(tokens, -1)
    rows, blocks = gate(rows, blocks)
    rows_other = flip(rows, "c")
    boundary = jnp.concatenate(
        [jnp.where(core == 0, rows, rows_other), jnp.where(core == 0, rows_other, rows)]
    )
    bound = exchange(blocks, TOK)

    wide_hidden_grad = dot(boundary, wide_down, ((1,), (1,)))
    wide_pre_grad = (wide_hidden_grad * silu_slope(wide_pre)).astype(BF16)
    wide_pre_grad, got = gate(wide_pre_grad, got)
    grad_rows = z_rows(wide_pre_grad)
    term_keep, term_send = term_blocks(wide_pre_grad, wide_up, core, half)
    term_send, in_blocks = gate(term_send, in_blocks)
    term_chip = (term_keep.astype(F32) + flip(term_send, "c").astype(F32)).astype(BF16)
    in_own = exchange(in_blocks, CHIPS).reshape(n_d * tokens, side)
    term_chip, bound_other, narrow_down_grad = gate(term_chip, flip(bound, "c"), narrow_down_grad)
    term_all = exchange(term_chip, CHIPS)

    other = flip(got, "c")
    mine = cut(wide_input, (yl * 4 + z) * side, side, 1)
    pair = cut(wide_input, ((1 - yl) * 4 + z) * side, side, 1)
    input_own = jnp.concatenate([mine, jnp.where(core == 0, got, other)])
    input_pair = jnp.concatenate([pair, jnp.where(core == 0, other, got)])
    up_send = dot(input_pair, grad_rows, ((0,), (0,))).astype(BF16)
    up_come = flip(up_send, "yl")

    bound = jnp.stack(
        [jnp.where(core == 0, bound, bound_other), jnp.where(core == 0, bound_other, bound)], axis=1
    ).reshape(-1, side)
    wide_down_grad = dot(act_all, bound, ((0,), (0,))).astype(BF16)

    wide_down_grad, in_own = gate(wide_down_grad, in_own)
    up_part = dot(in_own, pre_all, ((0,), (0,)))
    narrow_send = cut(up_part, (1 - core) * half, half, 0).astype(BF16)
    narrow_keep = cut(up_part, core * half, half, 0)
    narrow_up_grad = (narrow_keep + flip(narrow_send, "c").astype(F32)).astype(BF16)

    up_come, wide_down_grad, narrow_up_grad = gate(up_come, wide_down_grad, narrow_up_grad)
    wide_up_grad = (dot(input_own, grad_rows, ((0,), (0,))) + up_come.astype(F32)).astype(BF16)
    own_cols = cut(boundary, (chip * 2 + core) * half, half, 1)
    wide_up_grad, own_cols = gate(wide_up_grad, own_cols)
    wide_input_grad = (own_cols.astype(F32) + jnp.sum(term_all.astype(F32), axis=0)).astype(BF16)
    return (wide_input_grad, wide_up_grad, wide_down_grad, narrow_up_grad, narrow_down_grad)


def solution(mesh):
    fine = Mesh(mesh.devices.reshape(4, 2, 2, 2, 4), ("x", "yh", "c", "yl", "z"))
    dp = ("x", "yh", "c")
    tensor = ("yl", "z")
    in_specs = (
        P(None, dp),
        P(dp, None),
        P(dp, tensor),
        P(tensor, dp),
        P(tensor, None),
        P(tensor, dp),
        P(dp, None),
        P(dp, tensor),
        P(dp, tensor),
    )
    out_specs = (
        P(tensor, dp),
        P(tensor, dp),
        P(dp, tensor),
        P(dp, tensor),
        P(tensor, dp),
    )
    return jax.shard_map(body, mesh=fine, in_specs=in_specs, out_specs=out_specs, check_vma=False)
```
